32 devices in a mesh: layer: 2 (over x), row: 4 (over y, core), col: 4 (over z).
Axes of the slice: x: 2, y: 2, z: 4, core: 2. Of those that a mesh axis runs over, the one named last changes fastest.
Arguments:
- matrix: float32 [16384, 16384], P('row', 'col'), may hold values from -1.5 to 1.5, as said below
Outputs:
- square_panel: float32 [16384, 512], P('row', 'layer')
- new_panel: float32 [16384, 512], P('row', 'layer')
The draws below stay inside these ranges and needn't reach their ends.
Inputs may be any that keep to these rules, and one draw needn't show every extreme that they name: `matrix`: entries off the diagonal are of order 0.5 / sqrt(16384); the diagonal's magnitudes lie between 0.6 and 1 with either sign.
All inputs are finite; a program needn't handle non-finite values.
Results may differ from the reference program's by a relative error of at most 0.000076.
Values sent between devices are 32-bit elements; how exact they have to be, the bound alone decides.
No kernel may reach another device: no remote copies, remote signals or barrier semaphores. Data moves between devices by JAX's collectives and lax.ppermute only.
A program may use at most 128 MiB of HBM per device.

```python
import jax
import jax.numpy as jnp
from jax import lax

N = 16384
PW = 512


def draw_matrix(key, part):
    key_off = jax.random.fold_in(key, 11)
    key_mag = jax.random.fold_in(key, 12)
    key_sign = jax.random.fold_in(key, 13)
    entries = jax.random.normal(key_off, (N, N), jnp.float32)
    entries = entries * (0.5 / jnp.sqrt(jnp.float32(N)))
    magnitude = jax.random.uniform(key_mag, (N,), jnp.float32, 0.6, 1.0)
    signs = (2 * jax.random.randint(key_sign, (N,), 0, 2) - 1).astype(jnp.float32)
    diagonal_index = jnp.arange(N)
    entries = entries.at[diagonal_index, diagonal_index].add(magnitude * signs)
    return entries


def setup_inputs(seed: int = 0) -> dict:
    keys = jax.random.split(jax.random.key(seed), 2)
    matrix = draw_matrix(jax.random.fold_in(keys[1], 71), 0)
    return dict(matrix=matrix)


def matmul_high(left_side, right_side):
    return jnp.dot(left_side, right_side, precision=lax.Precision.HIGHEST, preferred_element_type=jnp.float32)


def reference(matrix):
    panel_block = matrix[:, :PW]
    square_panel = matmul_high(matrix, panel_block)
    update = matmul_high(matrix, square_panel)
    new_panel = (3.0 * panel_block - update) * 0.5
    return square_panel, new_panel
```

```python
import functools

import jax
import jax.numpy as jnp
from jax import lax
from jax.experimental import pallas as pl
from jax.experimental.pallas import tpu as pltpu
from jax.sharding import PartitionSpec as P

PW = 512
PANELS = 2
PIECES = 4
AHEAD = 2
AHEAD_LAST = 2
SHORT_LAST = True
HEADS = True
DETOUR = True
TILE = 512
KERNEL_VMEM = 40 * 1024 * 1024


def from_root(shard, axis, root):
    mine = lax.axis_index(axis) == root
    return lax.psum(jnp.where(mine, shard, jnp.zeros_like(shard)), axis)


def matmul_high(left_side, right_side):
    return jnp.dot(
        left_side, right_side, precision=lax.Precision.HIGHEST, preferred_element_type=jnp.float32
    )


def general_body(matrix):
    block_cols = matrix.shape[1]
    layers = lax.axis_size("layer")
    col_ratio = lax.axis_size("col") // lax.axis_size("row")
    col_index = lax.axis_index("col")
    layer_index = lax.axis_index("layer")
    half_width = PW // layers
    root_row = col_index // col_ratio
    offset = col_index % col_ratio * block_cols
    layer_slice = lax.dynamic_slice_in_dim(matrix[:, :PW], layer_index * half_width, half_width, 1)
    own_cols = from_root(layer_slice, "col", 0)
    panel_slab = from_root(
        lax.dynamic_slice_in_dim(own_cols, offset, block_cols, 0), "row", root_row
    )
    square = lax.psum(matmul_high(matrix, panel_slab), "col")
    square_slab = from_root(
        lax.dynamic_slice_in_dim(square, offset, block_cols, 0), "row", root_row
    )
    update = lax.psum(matmul_high(matrix, square_slab), "col")
    new_panel = (3.0 * own_cols - update) * 0.5
    return (square, new_panel)


class Order:
    token = None

    def call(self, body, args, in_specs, **settings):
        if self.token is None:
            kernel = body
        else:
            kernel = lambda _, *refs: body(*refs)
            args = [self.token, *args]
            in_specs = [pl.BlockSpec(memory_space=pl.ANY), *in_specs]
            aliases = settings.pop("input_output_aliases", {})
            settings["input_output_aliases"] = {i + 1: o for i, o in aliases.items()}
        out = pl.pallas_call(kernel, in_specs=in_specs, **settings, **LIGHT)(*args)
        self.token = out[0] if isinstance(out, (list, tuple)) else out
        return out


LIGHT = dict(
    compiler_params=pltpu.CompilerParams(vmem_limit_bytes=KERNEL_VMEM),
    cost_estimate=pl.CostEstimate(flops=1, bytes_accessed=1, transcendentals=0),
)
WHOLE = pl.BlockSpec(memory_space=pltpu.VMEM)
FLAG = pl.BlockSpec(memory_space=pltpu.SMEM)


def add_kernel(a_ref, b_ref, o_ref):
    o_ref[...] = a_ref[...] + b_ref[...]


def add(order, a, b):
    return order.call(
        add_kernel,
        [a, b],
        [WHOLE, WHOLE],
        out_specs=WHOLE,
        out_shape=jax.ShapeDtypeStruct(a.shape, a.dtype),
    )


def pick_kernel(flag_ref, a_ref, b_ref, o_ref):
    @pl.when(flag_ref[0] == 1)
    def _():
        o_ref[...] = a_ref[...]

    @pl.when(flag_ref[0] != 1)
    def _():
        o_ref[...] = b_ref[...]


def pick(order, flag, a, b):
    return order.call(
        pick_kernel,
        [flag, a, b],
        [FLAG, WHOLE, WHOLE],
        out_specs=WHOLE,
        out_shape=jax.ShapeDtypeStruct(a.shape, a.dtype),
    )


def store_kernel(flag_ref, a_ref, b_ref, *refs):
    o_ref, whole_ref = refs[-2:]

    @pl.when(flag_ref[0] == 1)
    def _():
        o_ref[...] = a_ref[...]
        whole_ref[...] = a_ref[...]

    @pl.when(flag_ref[0] != 1)
    def _():
        o_ref[...] = b_ref[...]
        whole_ref[...] = b_ref[...]


def pick_and_store(order, flag, a, b, whole, shape, place):
    block = pl.BlockSpec(a.shape, lambda i: (0, 0))
    earlier = [] if whole is None else [whole]
    return order.call(
        store_kernel,
        [flag, a, b, *earlier],
        [FLAG, block, block] + [pl.BlockSpec(memory_space=pl.ANY)] * len(earlier),
        grid=(1,),
        out_specs=[block, pl.BlockSpec(a.shape, lambda i: place)],
        out_shape=[
            jax.ShapeDtypeStruct(a.shape, a.dtype),
            jax.ShapeDtypeStruct(shape, a.dtype),
        ],
        input_output_aliases={3: 1} if earlier else {},
    )


def split_kernel(groups, count, *refs):
    flags, refs, w_ref = refs[:groups], refs[groups:-1], refs[-1]
    height, width = refs[0].shape

    def write(block, i):
        rows = pl.ds(i * height, height)
        high = block.astype(jnp.bfloat16)
        w_ref[rows, :width] = high
        w_ref[rows, width:] = (block - high.astype(jnp.float32)).astype(jnp.bfloat16)

    for i in range(count):
        flag_ref = flags[i * groups // count]

        @pl.when(flag_ref[0] == 1)
        def _():
            write(refs[i][...], i)

        @pl.when(flag_ref[0] != 1)
        def _():
            write(refs[count + i][...], i)


def pick_and_split(order, flags, left, right):
    height, width = left[0].shape
    count = len(left)
    return order.call(
        functools.partial(split_kernel, len(flags), count),
        [*flags, *left, *right],
        [FLAG] * len(flags) + [WHOLE] * (2 * count),
        out_specs=WHOLE,
        out_shape=jax.ShapeDtypeStruct((count * height, 2 * width), jnp.bfloat16),
    )


def product(x, w_ref):
    high = x.astype(jnp.bfloat16)
    low = (x - high.astype(jnp.float32)).astype(jnp.bfloat16)
    width = w_ref.shape[1] // 2
    total = jnp.dot(high, w_ref[...], preferred_element_type=jnp.float32)
    total = total[:, :width] + total[:, width:]
    return total + jnp.dot(low, w_ref[:, :width], preferred_element_type=jnp.float32)


def square_kernel(x_ref, w_ref, *o_refs):
    total = product(x_ref[...], w_ref)
    width = o_refs[0].shape[1]
    for k, o_ref in enumerate(o_refs):
        o_ref[...] = total[:, k * width : (k + 1) * width]


def base_kernel(scale_ref, own_ref, o_ref):
    o_ref[...] = scale_ref[0] * own_ref[...]


def scaled(order, scale, own):
    height = own.shape[0] // PIECES
    block = pl.BlockSpec((height, own.shape[1]), lambda i: (i, 0))
    return order.call(
        base_kernel,
        [scale, own],
        [FLAG, block],
        grid=(PIECES,),
        out_specs=block,
        out_shape=jax.ShapeDtypeStruct(own.shape, own.dtype),
    )


def head_kernel(x_ref, w_ref, o_ref):
    o_ref[...] = product(x_ref[...], w_ref)


def update_kernel(x_ref, w_ref, base_ref, *refs):
    total = product(x_ref[...], w_ref)
    if len(refs) > 1:
        total += refs[0][...]
    refs[-1][...] = base_ref[...] - 0.5 * total


def row_blocks(matrix, start, height, part, depth):
    tile = min(TILE, height)
    block = pl.BlockSpec((tile, depth), lambda i: (start // tile + i, part))
    return tile, height // tile, block


def square_piece(order, matrix, weights, start, height):
    tile, steps, block = row_blocks(matrix, start, height, 0, matrix.shape[1])
    width = weights.shape[1] // 2 // PANELS
    return order.call(
        square_kernel,
        [matrix, weights],
        [block, WHOLE],
        grid=(steps,),
        out_specs=[pl.BlockSpec((tile, width), lambda i: (i, 0))] * PANELS,
        out_shape=[jax.ShapeDtypeStruct((height, width), jnp.float32)] * PANELS,
    )


def head_piece(order, matrix, weights, start, height):
    depth, width = weights.shape[0], weights.shape[1] // 2
    tile, steps, block = row_blocks(matrix, start, height, 0, depth)
    return order.call(
        head_kernel,
        [matrix, weights],
        [block, WHOLE],
        grid=(steps,),
        out_specs=pl.BlockSpec((tile, width), lambda i: (i, 0)),
        out_shape=jax.ShapeDtypeStruct((height, width), jnp.float32),
    )


def update_piece(order, matrix, weights, head, base, start, height, panel):
    depth, width = weights.shape[0], weights.shape[1] // 2
    part = 0 if head is None else 1
    tile, steps, block = row_blocks(matrix, start, height, part, depth)
    local = pl.BlockSpec((tile, width), lambda i: (i, 0))
    extra = [] if head is None else [head]
    return order.call(
        update_kernel,
        [matrix, weights, base, *extra],
        [
            block,
            WHOLE,
            pl.BlockSpec((tile, width), lambda i: (start // tile + i, panel)),
            *([local] * len(extra)),
        ],
        grid=(steps,),
        out_specs=local,
        out_shape=jax.ShapeDtypeStruct((height, width), jnp.float32),
    )


def line_body(matrix):
    block_rows, block_cols = matrix.shape
    layers, rows, cols = (lax.axis_size(a) for a in ("layer", "row", "col"))
    layer, row, col = (lax.axis_index(a) for a in ("layer", "row", "col"))
    width = PW // layers // PANELS
    height = block_rows // PIECES
    both = ("row", "col")
    far = rows // 2
    flag = lambda mask: mask.astype(jnp.int32).reshape(1)
    middle = flag((col == 1) | (col == 2))
    source = flag(col == 0)
    inward = [(0, 1), (3, 2)]
    centre = [(1, 2), (2, 1)]
    outward = [(1, 0), (2, 3)]

    class Spread:
        def __init__(self, roots):
            at = lambda r, c: r * cols + c
            self.up = [(at(roots[c], 0), at(roots[c], c)) for c in range(1, cols)]
            self.across = [(at(roots[c], c), at(roots[c] ^ far, c)) for c in range(cols)]
            self.core = [
                (at(r, c), at(r ^ 1, c)) for c in range(cols) for r in (roots[c], roots[c] ^ far)
            ]
            here = functools.reduce(
                lambda total, c: jnp.where(col == c, roots[c], total), range(1, cols), roots[0]
            )
            self.first = flag(row == here)
            self.second = flag((row == here) | (row == (here ^ far)))

    home = Spread(list(range(cols)))
    detour = Spread(list(range(cols - 1)) + [0])

    order = Order()
    whole = (block_rows, PANELS * width)
    own = lax.dynamic_slice(matrix, (0, layer * whole[1]), whole)
    quarters = [slice(q * block_rows // 4, (q + 1) * block_rows // 4) for q in range(4)]
    climbs = [lax.ppermute(own[quarters[q]], both, home.up) for q in range(2)]
    sent = own[block_rows // 2 :]
    if DETOUR:
        moved = lax.ppermute(sent, both, [((cols - 1) * cols, 0)])
    ways = [home, home] + [detour if DETOUR else home] * 2
    steps = [None] * 4
    hops = [None] * 4

    def arrive(q):
        steps[q] = pick(order, source, own[quarters[q]], climbs[q])
        hops[q] = lax.ppermute(steps[q], both, ways[q].across)

    def cross(q):
        steps[q] = pick(order, ways[q].first, steps[q], hops[q])
        hops[q] = lax.ppermute(steps[q], both, ways[q].core)

    scale = jnp.where(col == 0, 1.5, 0.0).astype(jnp.float32).reshape(1)
    arrive(0)
    if DETOUR:
        sent = pick(order, flag(row == 0), moved, sent)
    half = block_rows // 4
    climbs += [lax.ppermute(sent[q * half : (q + 1) * half], both, ways[2].up) for q in range(2)]
    arrive(1)
    cross(0)
    arrive(2)
    cross(1)
    arrive(3)
    cross(2)
    cross(3)
    base = scaled(order, scale, own)

    pieces = [(k, p * height, height) for k in range(PANELS) for p in range(PIECES)]
    half_count = len(pieces)
    last = [(PANELS - 1, (PIECES - 1) * height + h * height // 2, height // 2) for h in range(2)]
    pieces = pieces + (pieces[:-1] + last if SHORT_LAST else pieces)
    count = len(pieces)
    seconds = [ways[0].second, ways[2].second]
    square_weights = pick_and_split(order, seconds, steps, hops)
    weights, heads = {}, {}
    partial, first, sums, second, totals, third, done = ([None] * count for _ in range(7))
    across, spread, core = ([None] * half_count for _ in range(3))
    outs = [None, None]

    def shared_weights(k, begin, end):
        part = slice(k * PIECES + begin, k * PIECES + end)
        return pick_and_split(order, [home.second], spread[part], core[part])

    def launch(g):
        k, start, size = pieces[g]
        if g >= half_count:
            if k not in weights:
                weights[k] = shared_weights(k, PIECES // 2 if heads.get(k) else 0, PIECES)
            head = heads[k][start // height] if heads.get(k) else None
            partial[g] = update_piece(
                order, matrix, weights[k], head, base, start, size, k
            )
        elif partial[g] is None:
            for other, block in enumerate(
                square_piece(order, matrix, square_weights, start, size)
            ):
                partial[other * PIECES + start // height] = block
        first[g] = lax.ppermute(partial[g], "col", inward)

    def can_launch(g):
        k = pieces[g][0]
        return g < half_count or shared >= (k + 1) * PIECES

    next_product = added = crossed = stored = shared = 0
    while next_product < AHEAD:
        launch(next_product)
        next_product += 1

    while stored < count:
        ready = (next_product, added, crossed, min(stored, half_count), shared)
        if added < ready[0]:
            g, added = added, added + 1
            sums[g] = add(order, partial[g], first[g])
            second[g] = lax.ppermute(sums[g], "col", centre)
        if crossed < ready[1]:
            g, crossed = crossed, crossed + 1
            totals[g] = add(order, sums[g], second[g])
            third[g] = lax.ppermute(totals[g], "col", outward)
        if stored < ready[2]:
            g, stored = stored, stored + 1
            k, start, size = pieces[g]
            kind = int(g >= half_count)
            done[g], outs[kind] = pick_and_store(
                order, middle, totals[g], third[g], outs[kind], whole, (start // size, k)
            )
            if kind == 0:
                across[g] = lax.ppermute(done[g], both, home.across)
        if shared < ready[3]:
            g, shared = shared, shared + 1
            spread[g] = pick(order, home.first, done[g], across[g])
            core[g] = lax.ppermute(spread[g], both, home.core)
        if HEADS and ready[4] >= PIECES // 2 and len(heads.setdefault(0, [])) < PIECES:
            if not heads[0]:
                head_weights = shared_weights(0, 0, PIECES // 2)
            for _ in range(2):
                start = len(heads[0]) * height
                heads[0].append(head_piece(order, matrix, head_weights, start, height))
        limit = AHEAD if next_product < half_count else AHEAD_LAST
        while next_product < min(count, added + limit) and can_launch(next_product):
            launch(next_product)
            next_product += 1

    return tuple(outs)


def solution(mesh):
    sizes = mesh.shape
    line = sizes["col"] == 4 and sizes["row"] == 4
    return jax.shard_map(
        line_body if line else general_body,
        mesh=mesh,
        in_specs=(P("row", "col"),),
        out_specs=(P("row", "layer"), P("row", "layer")),
        check_vma=False,
    )
```

```python
import functools

import jax
import jax.numpy as jnp
from jax import lax
from jax.experimental import pallas as pl
from jax.experimental.pallas import tpu as pltpu
from jax.sharding import PartitionSpec as P

PW = 512
PANELS = 2
PIECES = 4
AHEAD = 2
AHEAD_LAST = 2
SHORT_LAST = True
HEADS = False
DETOUR = True
TILE = 256
KERNEL_VMEM = 26 * 1024 * 1024


def from_root(shard, axis, root):
    mine = lax.axis_index(axis) == root
    return lax.psum(jnp.where(mine, shard, jnp.zeros_like(shard)), axis)


def matmul_high(left_side, right_side):
    return jnp.dot(
        left_side, right_side, precision=lax.Precision.HIGHEST, preferred_element_type=jnp.float32
    )


def general_body(matrix):
    block_cols = matrix.shape[1]
    layers = lax.axis_size("layer")
    col_ratio = lax.axis_size("col") // lax.axis_size("row")
    col_index = lax.axis_index("col")
    layer_index = lax.axis_index("layer")
    half_width = PW // layers
    root_row = col_index // col_ratio
    offset = col_index % col_ratio * block_cols
    layer_slice = lax.dynamic_slice_in_dim(matrix[:, :PW], layer_index * half_width, half_width, 1)
    own_cols = from_root(layer_slice, "col", 0)
    panel_slab = from_root(
        lax.dynamic_slice_in_dim(own_cols, offset, block_cols, 0), "row", root_row
    )
    square = lax.psum(matmul_high(matrix, panel_slab), "col")
    square_slab = from_root(
        lax.dynamic_slice_in_dim(square, offset, block_cols, 0), "row", root_row
    )
    update = lax.psum(matmul_high(matrix, square_slab), "col")
    new_panel = (3.0 * own_cols - update) * 0.5
    return (square, new_panel)


class Order:
    token = None

    def call(self, body, args, in_specs, **settings):
        if self.token is None:
            kernel = body
        else:
            kernel = lambda _, *refs: body(*refs)
            args = [self.token, *args]
            in_specs = [pl.BlockSpec(memory_space=pl.ANY), *in_specs]
            aliases = settings.pop("input_output_aliases", {})
            settings["input_output_aliases"] = {i + 1: o for i, o in aliases.items()}
        out = pl.pallas_call(kernel, in_specs=in_specs, **settings, **LIGHT)(*args)
        self.token = out[0] if isinstance(out, (list, tuple)) else out
        return out


LIGHT = dict(
    compiler_params=pltpu.CompilerParams(vmem_limit_bytes=KERNEL_VMEM),
    cost_estimate=pl.CostEstimate(flops=1, bytes_accessed=1, transcendentals=0),
)
WHOLE = pl.BlockSpec(memory_space=pltpu.VMEM)
FLAG = pl.BlockSpec(memory_space=pltpu.SMEM)


def add_kernel(a_ref, b_ref, o_ref):
    o_ref[...] = a_ref[...] + b_ref[...]


def add(order, a, b):
    return order.call(
        add_kernel,
        [a, b],
        [WHOLE, WHOLE],
        out_specs=WHOLE,
        out_shape=jax.ShapeDtypeStruct(a.shape, a.dtype),
    )


def pick_kernel(flag_ref, a_ref, b_ref, o_ref):
    @pl.when(flag_ref[0] == 1)
    def _():
        o_ref[...] = a_ref[...]

    @pl.when(flag_ref[0] != 1)
    def _():
        o_ref[...] = b_ref[...]


def pick(order, flag, a, b):
    return order.call(
        pick_kernel,
        [flag, a, b],
        [FLAG, WHOLE, WHOLE],
        out_specs=WHOLE,
        out_shape=jax.ShapeDtypeStruct(a.shape, a.dtype),
    )


def store_kernel(flag_ref, a_ref, b_ref, *refs):
    o_ref, whole_ref = refs[-2:]

    @pl.when(flag_ref[0] == 1)
    def _():
        o_ref[...] = a_ref[...]
        whole_ref[...] = a_ref[...]

    @pl.when(flag_ref[0] != 1)
    def _():
        o_ref[...] = b_ref[...]
        whole_ref[...] = b_ref[...]


def pick_and_store(order, flag, a, b, whole, shape, place):
    block = pl.BlockSpec(a.shape, lambda i: (0, 0))
    earlier = [] if whole is None else [whole]
    return order.call(
        store_kernel,
        [flag, a, b, *earlier],
        [FLAG, block, block] + [pl.BlockSpec(memory_space=pl.ANY)] * len(earlier),
        grid=(1,),
        out_specs=[block, pl.BlockSpec(a.shape, lambda i: place)],
        out_shape=[
            jax.ShapeDtypeStruct(a.shape, a.dtype),
            jax.ShapeDtypeStruct(shape, a.dtype),
        ],
        input_output_aliases={3: 1} if earlier else {},
    )


def split_kernel(groups, count, *refs):
    flags, refs, w_ref = refs[:groups], refs[groups:-1], refs[-1]
    height, width = refs[0].shape

    def write(block, i):
        rows = pl.ds(i * height, height)
        high = block.astype(jnp.bfloat16)
        w_ref[rows, :width] = high
        w_ref[rows, width:] = (block - high.astype(jnp.float32)).astype(jnp.bfloat16)

    for i in range(count):
        flag_ref = flags[i * groups // count]

        @pl.when(flag_ref[0] == 1)
        def _():
            write(refs[i][...], i)

        @pl.when(flag_ref[0] != 1)
        def _():
            write(refs[count + i][...], i)


def pick_and_split(order, flags, left, right):
    height, width = left[0].shape
    count = len(left)
    return order.call(
        functools.partial(split_kernel, len(flags), count),
        [*flags, *left, *right],
        [FLAG] * len(flags) + [WHOLE] * (2 * count),
        out_specs=WHOLE,
        out_shape=jax.ShapeDtypeStruct((count * height, 2 * width), jnp.bfloat16),
    )


def product(x, w_ref):
    high = x.astype(jnp.bfloat16)
    low = (x - high.astype(jnp.float32)).astype(jnp.bfloat16)
    width = w_ref.shape[1] // 2
    total = jnp.dot(high, w_ref[...], preferred_element_type=jnp.float32)
    total = total[:, :width] + total[:, width:]
    return total + jnp.dot(low, w_ref[:, :width], preferred_element_type=jnp.float32)


def square_kernel(x_ref, w_ref, *o_refs):
    total = product(x_ref[...], w_ref)
    width = o_refs[0].shape[1]
    for k, o_ref in enumerate(o_refs):
        o_ref[...] = total[:, k * width : (k + 1) * width]


def base_kernel(scale_ref, own_ref, o_ref):
    o_ref[...] = scale_ref[0] * own_ref[...]


def scaled(order, scale, own):
    height = own.shape[0] // PIECES
    block = pl.BlockSpec((height, own.shape[1]), lambda i: (i, 0))
    return order.call(
        base_kernel,
        [scale, own],
        [FLAG, block],
        grid=(PIECES,),
        out_specs=block,
        out_shape=jax.ShapeDtypeStruct(own.shape, own.dtype),
    )


def head_kernel(x_ref, w_ref, o_ref):
    o_ref[...] = product(x_ref[...], w_ref)


def update_kernel(x_ref, w_ref, base_ref, *refs):
    total = product(x_ref[...], w_ref)
    if len(refs) > 1:
        total += refs[0][...]
    refs[-1][...] = base_ref[...] - 0.5 * total


def row_blocks(matrix, start, height, part, depth):
    tile = min(TILE, height)
    block = pl.BlockSpec((tile, depth), lambda i: (start // tile + i, part))
    return tile, height // tile, block


def square_piece(order, matrix, weights, start, height):
    tile, steps, block = row_blocks(matrix, start, height, 0, matrix.shape[1])
    width = weights.shape[1] // 2 // PANELS
    return order.call(
        square_kernel,
        [matrix, weights],
        [block, WHOLE],
        grid=(steps,),
        out_specs=[pl.BlockSpec((tile, width), lambda i: (i, 0))] * PANELS,
        out_shape=[jax.ShapeDtypeStruct((height, width), jnp.float32)] * PANELS,
    )


def head_piece(order, matrix, weights, start, height):
    depth, width = weights.shape[0], weights.shape[1] // 2
    tile, steps, block = row_blocks(matrix, start, height, 0, depth)
    return order.call(
        head_kernel,
        [matrix, weights],
        [block, WHOLE],
        grid=(steps,),
        out_specs=pl.BlockSpec((tile, width), lambda i: (i, 0)),
        out_shape=jax.ShapeDtypeStruct((height, width), jnp.float32),
    )


def update_piece(order, matrix, weights, head, base, start, height, panel):
    depth, width = weights.shape[0], weights.shape[1] // 2
    part = 0 if head is None else 1
    tile, steps, block = row_blocks(matrix, start, height, part, depth)
    local = pl.BlockSpec((tile, width), lambda i: (i, 0))
    extra = [] if head is None else [head]
    return order.call(
        update_kernel,
        [matrix, weights, base, *extra],
        [
            block,
            WHOLE,
            pl.BlockSpec((tile, width), lambda i: (start // tile + i, panel)),
            *([local] * len(extra)),
        ],
        grid=(steps,),
        out_specs=local,
        out_shape=jax.ShapeDtypeStruct((height, width), jnp.float32),
    )


def line_body(matrix):
    block_rows, block_cols = matrix.shape
    layers, rows, cols = (lax.axis_size(a) for a in ("layer", "row", "col"))
    layer, row, col = (lax.axis_index(a) for a in ("layer", "row", "col"))
    width = PW // layers // PANELS
    height = block_rows // PIECES
    both = ("row", "col")
    far = rows // 2
    flag = lambda mask: mask.astype(jnp.int32).reshape(1)
    middle = flag((col == 1) | (col == 2))
    source = flag(col == 0)
    inward = [(0, 1), (3, 2)]
    centre = [(1, 2), (2, 1)]
    outward = [(1, 0), (2, 3)]

    class Spread:
        def __init__(self, roots):
            at = lambda r, c: r * cols + c
            self.up = [(at(roots[c], 0), at(roots[c], c)) for c in range(1, cols)]
            self.across = [(at(roots[c], c), at(roots[c] ^ far, c)) for c in range(cols)]
            self.core = [
                (at(r, c), at(r ^ 1, c)) for c in range(cols) for r in (roots[c], roots[c] ^ far)
            ]
            here = functools.reduce(
                lambda total, c: jnp.where(col == c, roots[c], total), range(1, cols), roots[0]
            )
            self.first = flag(row == here)
            self.second = flag((row == here) | (row == (here ^ far)))

    home = Spread(list(range(cols)))
    detour = Spread(list(range(cols - 1)) + [0])

    order = Order()
    whole = (block_rows, PANELS * width)
    own = lax.dynamic_slice(matrix, (0, layer * whole[1]), whole)
    quarters = [slice(q * block_rows // 4, (q + 1) * block_rows // 4) for q in range(4)]
    climbs = [lax.ppermute(own[quarters[q]], both, home.up) for q in range(2)]
    sent = own[block_rows // 2 :]
    if DETOUR:
        moved = lax.ppermute(sent, both, [((cols - 1) * cols, 0)])
    ways = [home, home] + [detour if DETOUR else home] * 2
    steps = [None] * 4
    hops = [None] * 4

    def arrive(q):
        steps[q] = pick(order, source, own[quarters[q]], climbs[q])
        hops[q] = lax.ppermute(steps[q], both, ways[q].across)

    def cross(q):
        steps[q] = pick(order, ways[q].first, steps[q], hops[q])
        hops[q] = lax.ppermute(steps[q], both, ways[q].core)

    scale = jnp.where(col == 0, 1.5, 0.0).astype(jnp.float32).reshape(1)
    arrive(0)
    if DETOUR:
        sent = pick(order, flag(row == 0), moved, sent)
    half = block_rows // 4
    climbs += [lax.ppermute(sent[q * half : (q + 1) * half], both, ways[2].up) for q in range(2)]
    arrive(1)
    cross(0)
    arrive(2)
    cross(1)
    arrive(3)
    cross(2)
    cross(3)
    base = scaled(order, scale, own)

    pieces = [(k, p * height, height) for k in range(PANELS) for p in range(PIECES)]
    half_count = len(pieces)
    last = [(PANELS - 1, (PIECES - 1) * height + h * height // 2, height // 2) for h in range(2)]
    pieces = pieces + (pieces[:-1] + last if SHORT_LAST else pieces)
    count = len(pieces)
    seconds = [ways[0].second, ways[2].second]
    square_weights = pick_and_split(order, seconds, steps, hops)
    weights, heads = {}, {}
    partial, first, sums, second, totals, third, done = ([None] * count for _ in range(7))
    across, spread, core = ([None] * half_count for _ in range(3))
    outs = [None, None]

    def shared_weights(k, begin, end):
        part = slice(k * PIECES + begin, k * PIECES + end)
        return pick_and_split(order, [home.second], spread[part], core[part])

    def launch(g):
        k, start, size = pieces[g]
        if g >= half_count:
            if k not in weights:
                weights[k] = shared_weights(k, PIECES // 2 if heads.get(k) else 0, PIECES)
            head = heads[k][start // height] if heads.get(k) else None
            partial[g] = update_piece(
                order, matrix, weights[k], head, base, start, size, k
            )
        elif partial[g] is None:
            for other, block in enumerate(
                square_piece(order, matrix, square_weights, start, size)
            ):
                partial[other * PIECES + start // height] = block
        first[g] = lax.ppermute(partial[g], "col", inward)

    def can_launch(g):
        k = pieces[g][0]
        return g < half_count or shared >= (k + 1) * PIECES

    next_product = added = crossed = stored = shared = 0
    while next_product < AHEAD:
        launch(next_product)
        next_product += 1

    while stored < count:
        ready = (next_product, added, crossed, min(stored, half_count), shared)
        if added < ready[0]:
            g, added = added, added + 1
            sums[g] = add(order, partial[g], first[g])
            second[g] = lax.ppermute(sums[g], "col", centre)
        if crossed < ready[1]:
            g, crossed = crossed, crossed + 1
            totals[g] = add(order, sums[g], second[g])
            third[g] = lax.ppermute(totals[g], "col", outward)
        if stored < ready[2]:
            g, stored = stored, stored + 1
            k, start, size = pieces[g]
            kind = int(g >= half_count)
            done[g], outs[kind] = pick_and_store(
                order, middle, totals[g], third[g], outs[kind], whole, (start // size, k)
            )
            if kind == 0:
                across[g] = lax.ppermute(done[g], both, home.across)
        if shared < ready[3]:
            g, shared = shared, shared + 1
            spread[g] = pick(order, home.first, done[g], across[g])
            core[g] = lax.ppermute(spread[g], both, home.core)
        if HEADS and ready[4] >= PIECES // 2 and len(heads.setdefault(0, [])) < PIECES:
            if not heads[0]:
                head_weights = shared_weights(0, 0, PIECES // 2)
            for _ in range(2):
                start = len(heads[0]) * height
                heads[0].append(head_piece(order, matrix, head_weights, start, height))
        limit = AHEAD if next_product < half_count else AHEAD_LAST
        while next_product < min(count, added + limit) and can_launch(next_product):
            launch(next_product)
            next_product += 1

    return tuple(outs)


def solution(mesh):
    sizes = mesh.shape
    line = sizes["col"] == 4 and sizes["row"] == 4
    return jax.shard_map(
        line_body if line else general_body,
        mesh=mesh,
        in_specs=(P("row", "col"),),
        out_specs=(P("row", "layer"), P("row", "layer")),
        check_vma=False,
    )
```

```python
import functools

import jax
import jax.numpy as jnp
from jax import lax
from jax.experimental import pallas as pl
from jax.experimental.pallas import tpu as pltpu
from jax.sharding import PartitionSpec as P

PW = 512
PANELS = 2
PIECES = 4
AHEAD = 2
AHEAD_LAST = 3
SHORT_LAST = True
HEADS = False
DETOUR = True
TILE = 256
KERNEL_VMEM = 26 * 1024 * 1024


def from_root(shard, axis, root):
    mine = lax.axis_index(axis) == root
    return lax.psum(jnp.where(mine, shard, jnp.zeros_like(shard)), axis)


def matmul_high(left_side, right_side):
    return jnp.dot(
        left_side, right_side, precision=lax.Precision.HIGHEST, preferred_element_type=jnp.float32
    )


def general_body(matrix):
    block_cols = matrix.shape[1]
    layers = lax.axis_size("layer")
    col_ratio = lax.axis_size("col") // lax.axis_size("row")
    col_index = lax.axis_index("col")
    layer_index = lax.axis_index("layer")
    half_width = PW // layers
    root_row = col_index // col_ratio
    offset = col_index % col_ratio * block_cols
    layer_slice = lax.dynamic_slice_in_dim(matrix[:, :PW], layer_index * half_width, half_width, 1)
    own_cols = from_root(layer_slice, "col", 0)
    panel_slab = from_root(
        lax.dynamic_slice_in_dim(own_cols, offset, block_cols, 0), "row", root_row
    )
    square = lax.psum(matmul_high(matrix, panel_slab), "col")
    square_slab = from_root(
        lax.dynamic_slice_in_dim(square, offset, block_cols, 0), "row", root_row
    )
    update = lax.psum(matmul_high(matrix, square_slab), "col")
    new_panel = (3.0 * own_cols - update) * 0.5
    return (square, new_panel)


class Order:
    token = None

    def call(self, body, args, in_specs, **settings):
        if self.token is None:
            kernel = body
        else:
            kernel = lambda _, *refs: body(*refs)
            args = [self.token, *args]
            in_specs = [pl.BlockSpec(memory_space=pl.ANY), *in_specs]
            aliases = settings.pop("input_output_aliases", {})
            settings["input_output_aliases"] = {i + 1: o for i, o in aliases.items()}
        out = pl.pallas_call(kernel, in_specs=in_specs, **settings, **LIGHT)(*args)
        self.token = out[0] if isinstance(out, (list, tuple)) else out
        return out


LIGHT = dict(
    compiler_params=pltpu.CompilerParams(vmem_limit_bytes=KERNEL_VMEM),
    cost_estimate=pl.CostEstimate(flops=1, bytes_accessed=1, transcendentals=0),
)
WHOLE = pl.BlockSpec(memory_space=pltpu.VMEM)
FLAG = pl.BlockSpec(memory_space=pltpu.SMEM)


def add_kernel(a_ref, b_ref, o_ref):
    o_ref[...] = a_ref[...] + b_ref[...]


def add(order, a, b):
    return order.call(
        add_kernel,
        [a, b],
        [WHOLE, WHOLE],
        out_specs=WHOLE,
        out_shape=jax.ShapeDtypeStruct(a.shape, a.dtype),
    )


def pick_kernel(flag_ref, a_ref, b_ref, o_ref):
    @pl.when(flag_ref[0] == 1)
    def _():
        o_ref[...] = a_ref[...]

    @pl.when(flag_ref[0] != 1)
    def _():
        o_ref[...] = b_ref[...]


def pick(order, flag, a, b):
    return order.call(
        pick_kernel,
        [flag, a, b],
        [FLAG, WHOLE, WHOLE],
        out_specs=WHOLE,
        out_shape=jax.ShapeDtypeStruct(a.shape, a.dtype),
    )


def store_kernel(flag_ref, a_ref, b_ref, *refs):
    o_ref, whole_ref = refs[-2:]

    @pl.when(flag_ref[0] == 1)
    def _():
        o_ref[...] = a_ref[...]
        whole_ref[...] = a_ref[...]

    @pl.when(flag_ref[0] != 1)
    def _():
        o_ref[...] = b_ref[...]
        whole_ref[...] = b_ref[...]


def pick_and_store(order, flag, a, b, whole, shape, place):
    block = pl.BlockSpec(a.shape, lambda i: (0, 0))
    earlier = [] if whole is None else [whole]
    return order.call(
        store_kernel,
        [flag, a, b, *earlier],
        [FLAG, block, block] + [pl.BlockSpec(memory_space=pl.ANY)] * len(earlier),
        grid=(1,),
        out_specs=[block, pl.BlockSpec(a.shape, lambda i: place)],
        out_shape=[
            jax.ShapeDtypeStruct(a.shape, a.dtype),
            jax.ShapeDtypeStruct(shape, a.dtype),
        ],
        input_output_aliases={3: 1} if earlier else {},
    )


def split_kernel(groups, count, *refs):
    flags, refs, w_ref = refs[:groups], refs[groups:-1], refs[-1]
    height, width = refs[0].shape

    def write(block, i):
        rows = pl.ds(i * height, height)
        high = block.astype(jnp.bfloat16)
        w_ref[rows, :width] = high
        w_ref[rows, width:] = (block - high.astype(jnp.float32)).astype(jnp.bfloat16)

    for i in range(count):
        flag_ref = flags[i * groups // count]

        @pl.when(flag_ref[0] == 1)
        def _():
            write(refs[i][...], i)

        @pl.when(flag_ref[0] != 1)
        def _():
            write(refs[count + i][...], i)


def pick_and_split(order, flags, left, right):
    height, width = left[0].shape
    count = len(left)
    return order.call(
        functools.partial(split_kernel, len(flags), count),
        [*flags, *left, *right],
        [FLAG] * len(flags) + [WHOLE] * (2 * count),
        out_specs=WHOLE,
        out_shape=jax.ShapeDtypeStruct((count * height, 2 * width), jnp.bfloat16),
    )


def product(x, w_ref):
    high = x.astype(jnp.bfloat16)
    low = (x - high.astype(jnp.float32)).astype(jnp.bfloat16)
    width = w_ref.shape[1] // 2
    total = jnp.dot(high, w_ref[...], preferred_element_type=jnp.float32)
    total = total[:, :width] + total[:, width:]
    return total + jnp.dot(low, w_ref[:, :width], preferred_element_type=jnp.float32)


def square_kernel(x_ref, w_ref, *o_refs):
    total = product(x_ref[...], w_ref)
    width = o_refs[0].shape[1]
    for k, o_ref in enumerate(o_refs):
        o_ref[...] = total[:, k * width : (k + 1) * width]


def base_kernel(scale_ref, own_ref, o_ref):
    o_ref[...] = scale_ref[0] * own_ref[...]


def scaled(order, scale, own):
    height = own.shape[0] // PIECES
    block = pl.BlockSpec((height, own.shape[1]), lambda i: (i, 0))
    return order.call(
        base_kernel,
        [scale, own],
        [FLAG, block],
        grid=(PIECES,),
        out_specs=block,
        out_shape=jax.ShapeDtypeStruct(own.shape, own.dtype),
    )


def head_kernel(x_ref, w_ref, o_ref):
    o_ref[...] = product(x_ref[...], w_ref)


def update_kernel(x_ref, w_ref, base_ref, *refs):
    total = product(x_ref[...], w_ref)
    if len(refs) > 1:
        total += refs[0][...]
    refs[-1][...] = base_ref[...] - 0.5 * total


def row_blocks(matrix, start, height, part, depth):
    tile = min(TILE, height)
    block = pl.BlockSpec((tile, depth), lambda i: (start // tile + i, part))
    return tile, height // tile, block


def square_piece(order, matrix, weights, start, height):
    tile, steps, block = row_blocks(matrix, start, height, 0, matrix.shape[1])
    width = weights.shape[1] // 2 // PANELS
    return order.call(
        square_kernel,
        [matrix, weights],
        [block, WHOLE],
        grid=(steps,),
        out_specs=[pl.BlockSpec((tile, width), lambda i: (i, 0))] * PANELS,
        out_shape=[jax.ShapeDtypeStruct((height, width), jnp.float32)] * PANELS,
    )


def head_piece(order, matrix, weights, start, height):
    depth, width = weights.shape[0], weights.shape[1] // 2
    tile, steps, block = row_blocks(matrix, start, height, 0, depth)
    return order.call(
        head_kernel,
        [matrix, weights],
        [block, WHOLE],
        grid=(steps,),
        out_specs=pl.BlockSpec((tile, width), lambda i: (i, 0)),
        out_shape=jax.ShapeDtypeStruct((height, width), jnp.float32),
    )


def update_piece(order, matrix, weights, head, base, start, height, panel):
    depth, width = weights.shape[0], weights.shape[1] // 2
    part = 0 if head is None else 1
    tile, steps, block = row_blocks(matrix, start, height, part, depth)
    local = pl.BlockSpec((tile, width), lambda i: (i, 0))
    extra = [] if head is None else [head]
    return order.call(
        update_kernel,
        [matrix, weights, base, *extra],
        [
            block,
            WHOLE,
            pl.BlockSpec((tile, width), lambda i: (start // tile + i, panel)),
            *([local] * len(extra)),
        ],
        grid=(steps,),
        out_specs=local,
        out_shape=jax.ShapeDtypeStruct((height, width), jnp.float32),
    )


def line_body(matrix):
    block_rows, block_cols = matrix.shape
    layers, rows, cols = (lax.axis_size(a) for a in ("layer", "row", "col"))
    layer, row, col = (lax.axis_index(a) for a in ("layer", "row", "col"))
    width = PW // layers // PANELS
    height = block_rows // PIECES
    both = ("row", "col")
    far = rows // 2
    flag = lambda mask: mask.astype(jnp.int32).reshape(1)
    middle = flag((col == 1) | (col == 2))
    source = flag(col == 0)
    inward = [(0, 1), (3, 2)]
    centre = [(1, 2), (2, 1)]
    outward = [(1, 0), (2, 3)]

    class Spread:
        def __init__(self, roots):
            at = lambda r, c: r * cols + c
            self.up = [(at(roots[c], 0), at(roots[c], c)) for c in range(1, cols)]
            self.across = [(at(roots[c], c), at(roots[c] ^ far, c)) for c in range(cols)]
            self.core = [
                (at(r, c), at(r ^ 1, c)) for c in range(cols) for r in (roots[c], roots[c] ^ far)
            ]
            here = functools.reduce(
                lambda total, c: jnp.where(col == c, roots[c], total), range(1, cols), roots[0]
            )
            self.first = flag(row == here)
            self.second = flag((row == here) | (row == (here ^ far)))

    home = Spread(list(range(cols)))
    detour = Spread(list(range(cols - 1)) + [0])

    order = Order()
    whole = (block_rows, PANELS * width)
    own = lax.dynamic_slice(matrix, (0, layer * whole[1]), whole)
    quarters = [slice(q * block_rows // 4, (q + 1) * block_rows // 4) for q in range(4)]
    climbs = [lax.ppermute(own[quarters[q]], both, home.up) for q in range(2)]
    sent = own[block_rows // 2 :]
    if DETOUR:
        moved = lax.ppermute(sent, both, [((cols - 1) * cols, 0)])
    ways = [home, home] + [detour if DETOUR else home] * 2
    steps = [None] * 4
    hops = [None] * 4

    def arrive(q):
        steps[q] = pick(order, source, own[quarters[q]], climbs[q])
        hops[q] = lax.ppermute(steps[q], both, ways[q].across)

    def cross(q):
        steps[q] = pick(order, ways[q].first, steps[q], hops[q])
        hops[q] = lax.ppermute(steps[q], both, ways[q].core)

    scale = jnp.where(col == 0, 1.5, 0.0).astype(jnp.float32).reshape(1)
    arrive(0)
    if DETOUR:
        sent = pick(order, flag(row == 0), moved, sent)
    half = block_rows // 4
    climbs += [lax.ppermute(sent[q * half : (q + 1) * half], both, ways[2].up) for q in range(2)]
    arrive(1)
    cross(0)
    arrive(2)
    cross(1)
    arrive(3)
    cross(2)
    cross(3)
    base = scaled(order, scale, own)

    pieces = [(k, p * height, height) for k in range(PANELS) for p in range(PIECES)]
    half_count = len(pieces)
    last = [(PANELS - 1, (PIECES - 1) * height + h * height // 2, height // 2) for h in range(2)]
    pieces = pieces + (pieces[:-1] + last if SHORT_LAST else pieces)
    count = len(pieces)
    seconds = [ways[0].second, ways[2].second]
    square_weights = pick_and_split(order, seconds, steps, hops)
    weights, heads = {}, {}
    partial, first, sums, second, totals, third, done = ([None] * count for _ in range(7))
    across, spread, core = ([None] * half_count for _ in range(3))
    outs = [None, None]

    def shared_weights(k, begin, end):
        part = slice(k * PIECES + begin, k * PIECES + end)
        return pick_and_split(order, [home.second], spread[part], core[part])

    def launch(g):
        k, start, size = pieces[g]
        if g >= half_count:
            if k not in weights:
                weights[k] = shared_weights(k, PIECES // 2 if heads.get(k) else 0, PIECES)
            head = heads[k][start // height] if heads.get(k) else None
            partial[g] = update_piece(
                order, matrix, weights[k], head, base, start, size, k
            )
        elif partial[g] is None:
            for other, block in enumerate(
                square_piece(order, matrix, square_weights, start, size)
            ):
                partial[other * PIECES + start // height] = block
        first[g] = lax.ppermute(partial[g], "col", inward)

    def can_launch(g):
        k = pieces[g][0]
        return g < half_count or shared >= (k + 1) * PIECES

    next_product = added = crossed = stored = shared = 0
    while next_product < AHEAD:
        launch(next_product)
        next_product += 1

    while stored < count:
        ready = (next_product, added, crossed, min(stored, half_count), shared)
        if added < ready[0]:
            g, added = added, added + 1
            sums[g] = add(order, partial[g], first[g])
            second[g] = lax.ppermute(sums[g], "col", centre)
        if crossed < ready[1]:
            g, crossed = crossed, crossed + 1
            totals[g] = add(order, sums[g], second[g])
            third[g] = lax.ppermute(totals[g], "col", outward)
        if stored < ready[2]:
            g, stored = stored, stored + 1
            k, start, size = pieces[g]
            kind = int(g >= half_count)
            done[g], outs[kind] = pick_and_store(
                order, middle, totals[g], third[g], outs[kind], whole, (start // size, k)
            )
            if kind == 0:
                across[g] = lax.ppermute(done[g], both, home.across)
        if shared < ready[3]:
            g, shared = shared, shared + 1
            spread[g] = pick(order, home.first, done[g], across[g])
            core[g] = lax.ppermute(spread[g], both, home.core)
        if HEADS and ready[4] >= PIECES // 2 and len(heads.setdefault(0, [])) < PIECES:
            if not heads[0]:
                head_weights = shared_weights(0, 0, PIECES // 2)
            for _ in range(2):
                start = len(heads[0]) * height
                heads[0].append(head_piece(order, matrix, head_weights, start, height))
        limit = AHEAD if next_product < half_count + PIECES else AHEAD_LAST
        while next_product < min(count, added + limit) and can_launch(next_product):
            launch(next_product)
            next_product += 1

    return tuple(outs)


def solution(mesh):
    sizes = mesh.shape
    line = sizes["col"] == 4 and sizes["row"] == 4
    return jax.shard_map(
        line_body if line else general_body,
        mesh=mesh,
        in_specs=(P("row", "col"),),
        out_specs=(P("row", "layer"), P("row", "layer")),
        check_vma=False,
    )
```

```python
import functools

import jax
import jax.numpy as jnp
from jax import lax
from jax.experimental import pallas as pl
from jax.experimental.pallas import tpu as pltpu
from jax.sharding import PartitionSpec as P

PW = 512
PANELS = 2
PIECES = 4
AHEAD = 2
AHEAD_LAST = 3
SHORT_LAST = True
HEADS = False
DETOUR = True
TILE = 256
KERNEL_VMEM = 22 * 1024 * 1024


def from_root(shard, axis, root):
    mine = lax.axis_index(axis) == root
    return lax.psum(jnp.where(mine, shard, jnp.zeros_like(shard)), axis)


def matmul_high(left_side, right_side):
    return jnp.dot(
        left_side, right_side, precision=lax.Precision.HIGHEST, preferred_element_type=jnp.float32
    )


def general_body(matrix):
    block_cols = matrix.shape[1]
    layers = lax.axis_size("layer")
    col_ratio = lax.axis_size("col") // lax.axis_size("row")
    col_index = lax.axis_index("col")
    layer_index = lax.axis_index("layer")
    half_width = PW // layers
    root_row = col_index // col_ratio
    offset = col_index % col_ratio * block_cols
    layer_slice = lax.dynamic_slice_in_dim(matrix[:, :PW], layer_index * half_width, half_width, 1)
    own_cols = from_root(layer_slice, "col", 0)
    panel_slab = from_root(
        lax.dynamic_slice_in_dim(own_cols, offset, block_cols, 0), "row", root_row
    )
    square = lax.psum(matmul_high(matrix, panel_slab), "col")
    square_slab = from_root(
        lax.dynamic_slice_in_dim(square, offset, block_cols, 0), "row", root_row
    )
    update = lax.psum(matmul_high(matrix, square_slab), "col")
    new_panel = (3.0 * own_cols - update) * 0.5
    return (square, new_panel)


class Order:
    token = None

    def call(self, body, args, in_specs, **settings):
        if self.token is None:
            kernel = body
        else:
            kernel = lambda _, *refs: body(*refs)
            args = [self.token, *args]
            in_specs = [pl.BlockSpec(memory_space=pl.ANY), *in_specs]
            aliases = settings.pop("input_output_aliases", {})
            settings["input_output_aliases"] = {i + 1: o for i, o in aliases.items()}
        out = pl.pallas_call(kernel, in_specs=in_specs, **settings, **LIGHT)(*args)
        self.token = out[0] if isinstance(out, (list, tuple)) else out
        return out


LIGHT = dict(
    compiler_params=pltpu.CompilerParams(vmem_limit_bytes=KERNEL_VMEM),
    cost_estimate=pl.CostEstimate(flops=1, bytes_accessed=1, transcendentals=0),
)
WHOLE = pl.BlockSpec(memory_space=pltpu.VMEM)
FLAG = pl.BlockSpec(memory_space=pltpu.SMEM)


def add_kernel(a_ref, b_ref, o_ref):
    o_ref[...] = a_ref[...] + b_ref[...]


def add(order, a, b):
    return order.call(
        add_kernel,
        [a, b],
        [WHOLE, WHOLE],
        out_specs=WHOLE,
        out_shape=jax.ShapeDtypeStruct(a.shape, a.dtype),
    )


def pick_kernel(flag_ref, a_ref, b_ref, o_ref):
    @pl.when(flag_ref[0] == 1)
    def _():
        o_ref[...] = a_ref[...]

    @pl.when(flag_ref[0] != 1)
    def _():
        o_ref[...] = b_ref[...]


def pick(order, flag, a, b):
    return order.call(
        pick_kernel,
        [flag, a, b],
        [FLAG, WHOLE, WHOLE],
        out_specs=WHOLE,
        out_shape=jax.ShapeDtypeStruct(a.shape, a.dtype),
    )


def store_kernel(flag_ref, a_ref, b_ref, *refs):
    o_ref, whole_ref = refs[-2:]

    @pl.when(flag_ref[0] == 1)
    def _():
        o_ref[...] = a_ref[...]
        whole_ref[...] = a_ref[...]

    @pl.when(flag_ref[0] != 1)
    def _():
        o_ref[...] = b_ref[...]
        whole_ref[...] = b_ref[...]


def pick_and_store(order, flag, a, b, whole, shape, place):
    block = pl.BlockSpec(a.shape, lambda i: (0, 0))
    earlier = [] if whole is None else [whole]
    return order.call(
        store_kernel,
        [flag, a, b, *earlier],
        [FLAG, block, block] + [pl.BlockSpec(memory_space=pl.ANY)] * len(earlier),
        grid=(1,),
        out_specs=[block, pl.BlockSpec(a.shape, lambda i: place)],
        out_shape=[
            jax.ShapeDtypeStruct(a.shape, a.dtype),
            jax.ShapeDtypeStruct(shape, a.dtype),
        ],
        input_output_aliases={3: 1} if earlier else {},
    )


def split_kernel(groups, count, *refs):
    flags, refs, w_ref = refs[:groups], refs[groups:-1], refs[-1]
    height, width = refs[0].shape

    def write(block, i):
        rows = pl.ds(i * height, height)
        high = block.astype(jnp.bfloat16)
        w_ref[rows, :width] = high
        w_ref[rows, width:] = (block - high.astype(jnp.float32)).astype(jnp.bfloat16)

    for i in range(count):
        flag_ref = flags[i * groups // count]

        @pl.when(flag_ref[0] == 1)
        def _():
            write(refs[i][...], i)

        @pl.when(flag_ref[0] != 1)
        def _():
            write(refs[count + i][...], i)


def pick_and_split(order, flags, left, right):
    height, width = left[0].shape
    count = len(left)
    return order.call(
        functools.partial(split_kernel, len(flags), count),
        [*flags, *left, *right],
        [FLAG] * len(flags) + [WHOLE] * (2 * count),
        out_specs=WHOLE,
        out_shape=jax.ShapeDtypeStruct((count * height, 2 * width), jnp.bfloat16),
    )


def product(x, w_ref):
    high = x.astype(jnp.bfloat16)
    low = (x - high.astype(jnp.float32)).astype(jnp.bfloat16)
    width = w_ref.shape[1] // 2
    total = jnp.dot(high, w_ref[...], preferred_element_type=jnp.float32)
    total = total[:, :width] + total[:, width:]
    return total + jnp.dot(low, w_ref[:, :width], preferred_element_type=jnp.float32)


def square_kernel(x_ref, w_ref, *o_refs):
    total = product(x_ref[...], w_ref)
    width = o_refs[0].shape[1]
    for k, o_ref in enumerate(o_refs):
        o_ref[...] = total[:, k * width : (k + 1) * width]


def base_kernel(scale_ref, own_ref, o_ref):
    o_ref[...] = scale_ref[0] * own_ref[...]


def scaled(order, scale, own):
    height = own.shape[0] // PIECES
    block = pl.BlockSpec((height, own.shape[1]), lambda i: (i, 0))
    return order.call(
        base_kernel,
        [scale, own],
        [FLAG, block],
        grid=(PIECES,),
        out_specs=block,
        out_shape=jax.ShapeDtypeStruct(own.shape, own.dtype),
    )


def head_kernel(x_ref, w_ref, o_ref):
    o_ref[...] = product(x_ref[...], w_ref)


def update_kernel(x_ref, w_ref, base_ref, *refs):
    total = product(x_ref[...], w_ref)
    if len(refs) > 1:
        total += refs[0][...]
    refs[-1][...] = base_ref[...] - 0.5 * total


def row_blocks(matrix, start, height, part, depth):
    tile = min(TILE, height)
    block = pl.BlockSpec((tile, depth), lambda i: (start // tile + i, part))
    return tile, height // tile, block


def square_piece(order, matrix, weights, start, height):
    tile, steps, block = row_blocks(matrix, start, height, 0, matrix.shape[1])
    width = weights.shape[1] // 2 // PANELS
    return order.call(
        square_kernel,
        [matrix, weights],
        [block, WHOLE],
        grid=(steps,),
        out_specs=[pl.BlockSpec((tile, width), lambda i: (i, 0))] * PANELS,
        out_shape=[jax.ShapeDtypeStruct((height, width), jnp.float32)] * PANELS,
    )


def head_piece(order, matrix, weights, start, height):
    depth, width = weights.shape[0], weights.shape[1] // 2
    tile, steps, block = row_blocks(matrix, start, height, 0, depth)
    return order.call(
        head_kernel,
        [matrix, weights],
        [block, WHOLE],
        grid=(steps,),
        out_specs=pl.BlockSpec((tile, width), lambda i: (i, 0)),
        out_shape=jax.ShapeDtypeStruct((height, width), jnp.float32),
    )


def update_piece(order, matrix, weights, head, base, start, height, panel):
    depth, width = weights.shape[0], weights.shape[1] // 2
    part = 0 if head is None else 1
    tile, steps, block = row_blocks(matrix, start, height, part, depth)
    local = pl.BlockSpec((tile, width), lambda i: (i, 0))
    extra = [] if head is None else [head]
    return order.call(
        update_kernel,
        [matrix, weights, base, *extra],
        [
            block,
            WHOLE,
            pl.BlockSpec((tile, width), lambda i: (start // tile + i, panel)),
            *([local] * len(extra)),
        ],
        grid=(steps,),
        out_specs=local,
        out_shape=jax.ShapeDtypeStruct((height, width), jnp.float32),
    )


def line_body(matrix):
    block_rows, block_cols = matrix.shape
    layers, rows, cols = (lax.axis_size(a) for a in ("layer", "row", "col"))
    layer, row, col = (lax.axis_index(a) for a in ("layer", "row", "col"))
    width = PW // layers // PANELS
    height = block_rows // PIECES
    both = ("row", "col")
    far = rows // 2
    flag = lambda mask: mask.astype(jnp.int32).reshape(1)
    middle = flag((col == 1) | (col == 2))
    source = flag(col == 0)
    inward = [(0, 1), (3, 2)]
    centre = [(1, 2), (2, 1)]
    outward = [(1, 0), (2, 3)]

    class Spread:
        def __init__(self, roots):
            at = lambda r, c: r * cols + c
            self.up = [(at(roots[c], 0), at(roots[c], c)) for c in range(1, cols)]
            self.across = [(at(roots[c], c), at(roots[c] ^ far, c)) for c in range(cols)]
            self.core = [
                (at(r, c), at(r ^ 1, c)) for c in range(cols) for r in (roots[c], roots[c] ^ far)
            ]
            here = functools.reduce(
                lambda total, c: jnp.where(col == c, roots[c], total), range(1, cols), roots[0]
            )
            self.first = flag(row == here)
            self.second = flag((row == here) | (row == (here ^ far)))

    home = Spread(list(range(cols)))
    detour = Spread(list(range(cols - 1)) + [0])

    order = Order()
    whole = (block_rows, PANELS * width)
    own = lax.dynamic_slice(matrix, (0, layer * whole[1]), whole)
    quarters = [slice(q * block_rows // 4, (q + 1) * block_rows // 4) for q in range(4)]
    climbs = [lax.ppermute(own[quarters[q]], both, home.up) for q in range(2)]
    sent = own[block_rows // 2 :]
    if DETOUR:
        moved = lax.ppermute(sent, both, [((cols - 1) * cols, 0)])
    ways = [home, home] + [detour if DETOUR else home] * 2
    steps = [None] * 4
    hops = [None] * 4

    def arrive(q):
        steps[q] = pick(order, source, own[quarters[q]], climbs[q])
        hops[q] = lax.ppermute(steps[q], both, ways[q].across)

    def cross(q):
        steps[q] = pick(order, ways[q].first, steps[q], hops[q])
        hops[q] = lax.ppermute(steps[q], both, ways[q].core)

    scale = jnp.where(col == 0, 1.5, 0.0).astype(jnp.float32).reshape(1)
    arrive(0)
    if DETOUR:
        sent = pick(order, flag(row == 0), moved, sent)
    half = block_rows // 4
    climbs += [lax.ppermute(sent[q * half : (q + 1) * half], both, ways[2].up) for q in range(2)]
    arrive(1)
    cross(0)
    arrive(2)
    cross(1)
    arrive(3)
    cross(2)
    cross(3)
    base = scaled(order, scale, own)

    pieces = [(k, p * height, height) for k in range(PANELS) for p in range(PIECES)]
    half_count = len(pieces)
    last = [(PANELS - 1, (PIECES - 1) * height + h * height // 2, height // 2) for h in range(2)]
    pieces = pieces + (pieces[:-1] + last if SHORT_LAST else pieces)
    count = len(pieces)
    seconds = [ways[0].second, ways[2].second]
    square_weights = pick_and_split(order, seconds, steps, hops)
    weights, heads = {}, {}
    partial, first, sums, second, totals, third, done = ([None] * count for _ in range(7))
    across, spread, core = ([None] * half_count for _ in range(3))
    outs = [None, None]

    def shared_weights(k, begin, end):
        part = slice(k * PIECES + begin, k * PIECES + end)
        return pick_and_split(order, [home.second], spread[part], core[part])

    def launch(g):
        k, start, size = pieces[g]
        if g >= half_count:
            if k not in weights:
                weights[k] = shared_weights(k, PIECES // 2 if heads.get(k) else 0, PIECES)
            head = heads[k][start // height] if heads.get(k) else None
            partial[g] = update_piece(
                order, matrix, weights[k], head, base, start, size, k
            )
        elif partial[g] is None:
            for other, block in enumerate(
                square_piece(order, matrix, square_weights, start, size)
            ):
                partial[other * PIECES + start // height] = block
        first[g] = lax.ppermute(partial[g], "col", inward)

    def can_launch(g):
        k = pieces[g][0]
        return g < half_count or shared >= (k + 1) * PIECES

    next_product = added = crossed = stored = shared = 0
    while next_product < AHEAD:
        launch(next_product)
        next_product += 1

    while stored < count:
        ready = (next_product, added, crossed, min(stored, half_count), shared)
        if added < ready[0]:
            g, added = added, added + 1
            sums[g] = add(order, partial[g], first[g])
            second[g] = lax.ppermute(sums[g], "col", centre)
        if crossed < ready[1]:
            g, crossed = crossed, crossed + 1
            totals[g] = add(order, sums[g], second[g])
            third[g] = lax.ppermute(totals[g], "col", outward)
        if stored < ready[2]:
            g, stored = stored, stored + 1
            k, start, size = pieces[g]
            kind = int(g >= half_count)
            done[g], outs[kind] = pick_and_store(
                order, middle, totals[g], third[g], outs[kind], whole, (start // size, k)
            )
            if kind == 0:
                across[g] = lax.ppermute(done[g], both, home.across)
        if shared < ready[3]:
            g, shared = shared, shared + 1
            spread[g] = pick(order, home.first, done[g], across[g])
            core[g] = lax.ppermute(spread[g], both, home.core)
        if HEADS and ready[4] >= PIECES // 2 and len(heads.setdefault(0, [])) < PIECES:
            if not heads[0]:
                head_weights = shared_weights(0, 0, PIECES // 2)
            for _ in range(2):
                start = len(heads[0]) * height
                heads[0].append(head_piece(order, matrix, head_weights, start, height))
        limit = AHEAD if next_product < half_count + PIECES else AHEAD_LAST
        while next_product < min(count, added + limit) and can_launch(next_product):
            launch(next_product)
            next_product += 1

    return tuple(outs)


def solution(mesh):
    sizes = mesh.shape
    line = sizes["col"] == 4 and sizes["row"] == 4
    return jax.shard_map(
        line_body if line else general_body,
        mesh=mesh,
        in_specs=(P("row", "col"),),
        out_specs=(P("row", "layer"), P("row", "layer")),
        check_vma=False,
    )
```
